256 devices in a mesh: gx: 8 (over z_lo, x), gy: 4 (over y), gz: 8 (over z_hi, core).
Axes of the slice: x: 4, y: 4, z: 8 (z_hi: 4, z_lo: 2; z = z_hi * 2 + z_lo), core: 2. Of those that a mesh axis runs over, the one named last changes fastest.
Arguments:
- normed: bfloat16 [4096, 3072], P(('gy', 'gx'), 'gz'), may hold values from -6 to 6
- out_grad: bfloat16 [4096, 3072], P(('gy', 'gx'), 'gz'), may hold values from -6 to 6
- projected: bfloat16 [4096, 9216], P('gy', 'gx'), may hold values from -5 to 5
- mixed_heads: bfloat16 [4096, 3072], P('gy', 'gx'), may hold values from -6 to 6
- hidden_pre: bfloat16 [4096, 12288], P('gy', 'gx'), may hold values from -6 to 6
- attend_in: bfloat16 [3072, 9216], P('gz', ('gx', 'gy')), may hold values from -0.109375 to 0.109375
- hidden_in: bfloat16 [3072, 12288], P('gz', ('gx', 'gy')), may hold values from -0.109375 to 0.109375
- attend_out: bfloat16 [3072, 3072], P(('gx', 'gy'), 'gz'), may hold values from -0.109375 to 0.109375
- hidden_out: bfloat16 [12288, 3072], P(('gx', 'gy'), 'gz'), may hold values from -0.0546875 to 0.0546875
Outputs:
- normed_grad: bfloat16 [4096, 3072], P(('gy', 'gx'), 'gz')
- attend_in_grad: bfloat16 [3072, 9216], P('gz', ('gx', 'gy'))
- hidden_in_grad: bfloat16 [3072, 12288], P('gz', ('gx', 'gy'))
- attend_out_grad: bfloat16 [3072, 3072], P(('gx', 'gy'), 'gz')
- hidden_out_grad: bfloat16 [12288, 3072], P(('gx', 'gy'), 'gz')
The draws below stay inside these ranges and needn't reach their ends.
All inputs are finite; a program needn't handle non-finite values.
Results may differ from the reference program's by a relative error of at most 0.02.
Values may be sent and summed in bfloat16 or wider, within the bound.
No kernel may reach another device: no remote copies, remote signals or barrier semaphores. Data moves between devices by JAX's collectives and lax.ppermute only.
A program may use at most 128 MiB of HBM per device.

```python
import jax
import jax.numpy as jnp
from jax import lax

D = 3072
HEADS = 24
HEAD = 128
FF = 12288
LEN = 1024
IMAGES = 4
TOKENS = 4096
DA = 3072


def draw_projected(key, part):
    key = jax.random.fold_in(key, 11)
    first_key = jax.random.fold_in(key, 0)
    stacked = jnp.clip(jax.random.normal(first_key, (TOKENS, HEADS, 3, HEAD), jnp.float32), -5.0, 5.0)
    return stacked.reshape(TOKENS, 3 * HEADS * HEAD).astype(jnp.bfloat16)


def level_of(own_key, extent, cuts, low, high):
    def one(dim, parts):
        draws = jax.random.uniform(jax.random.fold_in(jax.random.fold_in(own_key, 6), dim), (parts,), jnp.float32, low / len(cuts), high / len(cuts))
        return jnp.repeat(jnp.exp(draws), extent[dim] // parts).reshape((-1,) + (1,) * (len(extent) - dim - 1))

    gain = one(*cuts[0])
    for cut in cuts[1:]:
        gain = gain * one(*cut)
    return gain


def normal_values(stream_key, shape, width, most, shards=(), kind=jnp.bfloat16):
    drawn = jax.random.normal(stream_key, shape, jnp.float32) * width
    if len(shards) > 0:
        drawn = level_of(stream_key, shape, shards, -0.22, 0.18) * drawn
    return jnp.clip(drawn, min=-most, max=most).astype(kind)


def setup_inputs(seed: int = 0) -> dict:
    key_of = jax.random.split(jax.random.key(seed), 10)
    return {
        "normed": normal_values(key_of[0], (TOKENS, D), 1.0, 6.0, ((0, 32), (1, 8))),
        "out_grad": normal_values(key_of[1], (TOKENS, D), 1.0, 6.0, ((0, 32), (1, 8))),
        "projected": draw_projected(jax.random.fold_in(key_of[9], 71), 0),
        "mixed_heads": normal_values(key_of[3], (TOKENS, DA), 1.0, 6.0, ((0, 4), (1, 8))),
        "hidden_pre": normal_values(key_of[4], (TOKENS, FF), 1.0, 6.0, ((0, 4), (1, 8))),
        "attend_in": normal_values(key_of[5], (D, 3 * DA), D ** -0.5, 0.109375, ((0, 8), (1, 32))),
        "hidden_in": normal_values(key_of[6], (D, FF), D ** -0.5, 0.109375, ((0, 8), (1, 32))),
        "attend_out": normal_values(key_of[7], (DA, D), DA ** -0.5, 0.109375, ((0, 32), (1, 8))),
        "hidden_out": normal_values(key_of[8], (FF, D), FF ** -0.5, 0.0546875, ((0, 32), (1, 8))),
    }


def gelu_value(values):
    return 0.5 * values * (1.0 + lax.erf(values * 0.7071067811865476))


def gelu_slope(values):
    return 0.5 * (1.0 + lax.erf(values * 0.7071067811865476)) + values * jnp.exp(-0.5 * values * values) * 0.3989422804014327


def head_backward(inputs):
    queries, key_rows, value_rows, head_grad = inputs
    score_scale = HEAD ** -0.5
    scores = jnp.dot(queries, key_rows.T, preferred_element_type=jnp.float32) * score_scale
    largest = jnp.max(scores, axis=1, keepdims=True)
    weights = jnp.exp(scores - largest)
    probability = weights / jnp.sum(weights, axis=1, keepdims=True)
    value_grad = jnp.dot(probability.astype(jnp.bfloat16).T, head_grad, preferred_element_type=jnp.float32)
    prob_grad = jnp.dot(head_grad, value_rows.T, preferred_element_type=jnp.float32)
    centre = jnp.sum(probability * prob_grad, axis=1, keepdims=True)
    score_grad = (probability * (prob_grad - centre)).astype(jnp.bfloat16)
    query_grad = score_scale * jnp.dot(score_grad, key_rows, preferred_element_type=jnp.float32)
    key_grad = score_scale * jnp.dot(score_grad.T, queries, preferred_element_type=jnp.float32)
    return jnp.stack([query_grad, key_grad, value_grad], axis=1)


def reference(normed, out_grad, projected, mixed_heads, hidden_pre, attend_in, hidden_in, attend_out, hidden_out):
    merge_part = jnp.dot(out_grad, attend_out.T, preferred_element_type=jnp.float32)
    hidden_part = jnp.dot(out_grad, hidden_out.T, preferred_element_type=jnp.float32)
    heads_grad = merge_part.astype(jnp.bfloat16)
    pre_float = hidden_pre.astype(jnp.float32)
    hidden_grad = (hidden_part * gelu_slope(pre_float)).astype(jnp.bfloat16)
    activated = gelu_value(pre_float).astype(jnp.bfloat16)
    split_heads = projected.reshape(IMAGES, LEN, HEADS, 3, HEAD).transpose(2, 0, 3, 1, 4).reshape(
        HEADS * IMAGES, 3, LEN, HEAD)
    grads_heads = heads_grad.reshape(IMAGES, LEN, HEADS, HEAD).transpose(2, 0, 1, 3).reshape(
        HEADS * IMAGES, LEN, HEAD)
    stacked = lax.map(head_backward, (split_heads[:, 0], split_heads[:, 1], split_heads[:, 2], grads_heads))
    projected_grad = stacked.reshape(HEADS, IMAGES, LEN, 3, HEAD).transpose(1, 2, 0, 3, 4).reshape(
        TOKENS, 3 * DA).astype(jnp.bfloat16)
    normed_grad = (jnp.dot(projected_grad, attend_in.T, preferred_element_type=jnp.float32)
                   + jnp.dot(hidden_grad, hidden_in.T, preferred_element_type=jnp.float32)).astype(jnp.bfloat16)
    attend_in_grad = jnp.dot(normed.T, projected_grad, preferred_element_type=jnp.float32).astype(jnp.bfloat16)
    hidden_in_grad = jnp.dot(normed.T, hidden_grad, preferred_element_type=jnp.float32).astype(jnp.bfloat16)
    attend_out_grad = jnp.dot(mixed_heads.T, out_grad, preferred_element_type=jnp.float32).astype(jnp.bfloat16)
    hidden_out_grad = jnp.dot(activated.T, out_grad, preferred_element_type=jnp.float32).astype(jnp.bfloat16)
    return (normed_grad, attend_in_grad, hidden_in_grad, attend_out_grad, hidden_out_grad)
```

```python
import functools

import jax
import jax.numpy as jnp
from jax import lax
from jax.experimental import pallas as pl
from jax.experimental.pallas import tpu as pltpu
from jax.sharding import PartitionSpec as P

HEAD = 128
F32 = jnp.float32
BF16 = jnp.bfloat16
NT = (((1,), (1,)), ((), ()))
NN = (((1,), (0,)), ((), ()))
VMEM_LIMIT = 56 * 1024 * 1024

X_NEXT = [(i, i // 4 * 4 + (i + 3) % 4) for i in range(8)]
X_FAR = [(i, i // 4 * 4 + (i + 2) % 4) for i in range(8)]
X_PREV = [(i, i // 4 * 4 + (i + 1) % 4) for i in range(8)]
Z_LO = [(i, (i + 4) % 8) for i in range(8)]
Y_NEXT = [(i, (i + 3) % 4) for i in range(4)]
Y_FAR = [(i, (i + 2) % 4) for i in range(4)]
Y_PREV = [(i, (i + 1) % 4) for i in range(4)]
Z_NEXT = [(i, (i + 6) % 8) for i in range(8)]
Z_FAR = [(i, (i + 4) % 8) for i in range(8)]
Z_PREV = [(i, (i + 2) % 8) for i in range(8)]
CORE = [(i, i ^ 1) for i in range(8)]


def gelu_value(values):
    return 0.5 * values * (1.0 + lax.erf(values * 0.7071067811865476))


def gelu_slope(values):
    return (
        0.5 * (1.0 + lax.erf(values * 0.7071067811865476))
        + values * jnp.exp(-0.5 * values * values) * 0.3989422804014327
    )


def dot(a, b, dims):
    return lax.dot_general(a, b, dims, preferred_element_type=F32)


def from_others(value, axis, nxt, far, prv):
    return [
        value,
        lax.ppermute(value, axis, nxt),
        lax.ppermute(value, axis, far),
        lax.ppermute(value, axis, prv),
    ]


def whole(count):
    return [pl.BlockSpec(memory_space=pltpu.VMEM)] * count


def params(name=None):
    return pltpu.CompilerParams(vmem_limit_bytes=VMEM_LIMIT)


def assemble_body(place, *refs):
    pieces, (grad_ref, norm_ref, turned_ref) = refs[:8], refs[8:]
    for number in range(8):
        side, step = number // 4, number % 4
        index = lax.rem(place[1] + side, 2) * 4 + lax.rem(place[0] + step, 4)
        at = pl.ds(pl.multiple_of(index * 128, 128), 128)
        grad_ref[at, :] = pieces[number][:, :1536]
        rows = pieces[number][:, 1536:]
        norm_ref[at, :] = rows
        turned_ref[:, at] = rows.T


def assemble(place, pieces):
    return pl.pallas_call(
        assemble_body,
        in_specs=[pl.BlockSpec(memory_space=pltpu.SMEM)] + whole(8),
        out_specs=whole(3),
        out_shape=(
            jax.ShapeDtypeStruct((1024, 1536), BF16),
            jax.ShapeDtypeStruct((1024, 384), BF16),
            jax.ShapeDtypeStruct((384, 1024), BF16),
        ),
        compiler_params=params(),
        name="assemble",
    )(place, *pieces)


def hidden_body(grad_ref, first, middle, last, out_ref):
    total = dot(grad_ref[:, :384], first[:384, :], NT)
    total += dot(grad_ref[:, 384:1152], middle[:384, :], NT)
    total += dot(grad_ref[:, 1152:], last[:384, :], NT)
    out_ref[...] = total.astype(BF16)


def hidden_part(grads, first, middle, last):
    return pl.pallas_call(
        hidden_body,
        grid=(2,),
        in_specs=[pl.BlockSpec((512, 1536), lambda i: (i, 0))]
        + [
            pl.BlockSpec(w.shape, lambda i: (0, 0)) for w in (first, middle, last)
        ],
        out_specs=pl.BlockSpec((512, 384), lambda i: (i, 0)),
        out_shape=jax.ShapeDtypeStruct((1024, 384), BF16),
        compiler_params=params(),
        name="hidden_part",
    )(grads, first, middle, last)


def merge_body(place, grad_ref, *refs):
    weights, out_ref, held = refs[:12], refs[12], refs[13]
    for step in range(4):
        row = lax.rem(place[2] + step, 4) * 96
        at = pl.ds(pl.multiple_of(row, 32), 96)
        held[at, :384] = weights[3 * step][384:, :]
        held[at, 384:1152] = weights[3 * step + 1][384:, :]
        held[at, 1152:] = weights[3 * step + 2][384:, :]
    out_ref[...] = dot(grad_ref[...], held[...], NT).astype(BF16)


def merge_part(place, grads, weights):
    return pl.pallas_call(
        merge_body,
        in_specs=[pl.BlockSpec(memory_space=pltpu.SMEM)] + whole(13),
        out_specs=pl.BlockSpec(memory_space=pltpu.VMEM),
        out_shape=jax.ShapeDtypeStruct((1024, 384), BF16),
        scratch_shapes=[pltpu.VMEM((384, 1536), BF16)],
        compiler_params=params(),
        name="merge_part",
    )(place, grads, *weights)


SPAN = 256


def attend_body(rows_ref, mine_ref, other_ref, out_ref, key_sum, value_sum):
    scale = HEAD ** (-0.5)
    power = scale * 1.4426950408889634
    keys = rows_ref[:, HEAD : 2 * HEAD]
    values = rows_ref[:, 2 * HEAD :]
    turned = keys.T
    for part in range(1024 // SPAN):
        at = slice(part * SPAN, (part + 1) * SPAN)
        queries = rows_ref[at, :HEAD]
        grads = (mine_ref[at, :].astype(F32) + other_ref[at, :].astype(F32)).astype(BF16)
        scores = dot(keys, queries, NT)
        largest = jnp.max(scores, axis=0, keepdims=True)
        weights = jnp.exp2((scores - largest) * power)
        inverse = 1.0 / jnp.sum(weights, axis=0, keepdims=True)
        probability = weights * inverse
        prob_grad = dot(values, grads, NT)
        centre = jnp.sum(probability * prob_grad, axis=0, keepdims=True)
        score_grad = (probability * (prob_grad - centre)).astype(BF16)
        key_part = dot(score_grad, queries, NN)
        value_part = dot(probability.astype(BF16), grads, NN)
        if part == 0:
            key_sum[...] = key_part
            value_sum[...] = value_part
        else:
            key_sum[...] += key_part
            value_sum[...] += value_part
        query_grad = dot(turned, score_grad, NN) * scale
        out_ref[at, :HEAD] = query_grad.T.astype(BF16)
    out_ref[:, HEAD : 2 * HEAD] = (key_sum[...] * scale).astype(BF16)
    out_ref[:, 2 * HEAD :] = value_sum[...].astype(BF16)


def attend(projected, mine, other):
    heads = projected.shape[1] // (3 * HEAD)
    return pl.pallas_call(
        attend_body,
        grid=(heads,),
        in_specs=[
            pl.BlockSpec((1024, 3 * HEAD), lambda h: (0, h)),
            pl.BlockSpec((1024, HEAD), lambda h: (0, h)),
            pl.BlockSpec((1024, HEAD), lambda h: (0, h)),
        ],
        out_specs=pl.BlockSpec((1024, 3 * HEAD), lambda h: (0, h)),
        out_shape=jax.ShapeDtypeStruct(projected.shape, BF16),
        scratch_shapes=[pltpu.VMEM((1024, HEAD), F32)] * 2,
        compiler_params=params(),
        name="attend",
    )(projected, mine, other)


def slope_body(mine_ref, other_ref, slope_ref, turned_ref, grad_ref, out_ref):
    total = mine_ref[...].astype(F32) + other_ref[...].astype(F32)
    grad = (total * slope_ref[...].astype(F32)).astype(BF16)
    grad_ref[...] = grad
    out_ref[...] = dot(turned_ref[...], grad, NN).astype(BF16)


def hidden_step(place, step, mine, other, slope, turned):
    def wrapped(place_ref, *refs):
        slope_body(*refs)

    return pl.pallas_call(
        wrapped,
        grid_spec=pltpu.PrefetchScalarGridSpec(
            num_scalar_prefetch=1,
            grid=(1,),
            in_specs=[
                pl.BlockSpec((1024, 384), lambda i, p: (0, 0)),
                pl.BlockSpec((1024, 384), lambda i, p: (0, 0)),
                pl.BlockSpec((1024, 384), lambda i, p: (0, lax.rem(p[2] + step, 4))),
                pl.BlockSpec((384, 1024), lambda i, p: (0, 0)),
            ],
            out_specs=[
                pl.BlockSpec((1024, 384), lambda i, p: (0, 0)),
                pl.BlockSpec((384, 384), lambda i, p: (0, 0)),
            ],
        ),
        out_shape=(
            jax.ShapeDtypeStruct((1024, 384), BF16),
            jax.ShapeDtypeStruct((384, 384), BF16),
        ),
        compiler_params=params(),
        name=f"hidden_step",
    )(place, mine, other, slope, turned)


def input_body(place, *refs):
    attend_ref, weight_ref = refs[0], refs[1]
    hidden = refs[2:6]
    outs, held, rows = refs[6:10], refs[10], refs[11]
    for number in range(4):
        held[pl.ds(number * 288, 288), :] = weight_ref[number, 384:, :]
    total = dot(attend_ref[...], held[...], NN)
    for step in range(4):
        total += dot(hidden[step][...], weight_ref[lax.rem(place[2] + step, 4), :384, :], NT)
    rows[...] = total.astype(BF16)
    for step in range(4):
        for side in range(2):
            index = lax.rem(place[1] + side, 2) * 4 + lax.rem(place[0] + step, 4)
            at = pl.ds(pl.multiple_of(index * 128, 128), 128)
            outs[step][pl.ds(side * 128, 128), :] = rows[at, :]


def input_part(place, projected_grad, weights, hidden):
    return pl.pallas_call(
        input_body,
        in_specs=[pl.BlockSpec(memory_space=pltpu.SMEM)] + whole(6),
        out_specs=whole(4),
        out_shape=[jax.ShapeDtypeStruct((256, 384), BF16)] * 4,
        scratch_shapes=[pltpu.VMEM((1152, 384), BF16), pltpu.VMEM((1024, 384), BF16)],
        compiler_params=params(),
        name="input_part",
    )(place, projected_grad, weights, *hidden)


def local(
    normed,
    out_grad,
    projected,
    mixed_heads,
    hidden_pre,
    attend_in,
    hidden_in,
    attend_out,
    hidden_out,
):
    across = lax.axis_index("gx")
    place = jnp.stack([across % 4, across // 4, lax.axis_index("gy")]).astype(jnp.int32)

    weights = jnp.concatenate([hidden_out, attend_out], axis=0)
    w_next = lax.ppermute(weights, "gz", Z_NEXT)
    w_prev = lax.ppermute(weights, "gz", Z_PREV)
    firsts = from_others(weights, "gy", Y_NEXT, Y_FAR, Y_PREV)

    pieces = [out_grad] + [
        lax.ppermute(out_grad, "gz", perm) for perm in (Z_NEXT, Z_PREV, Z_FAR)
    ]
    row_piece = jnp.concatenate(pieces + [normed], axis=1)
    w_far = lax.ppermute(weights, "gz", Z_FAR)
    near_rows = from_others(row_piece, "gx", X_NEXT, X_FAR, X_PREV)
    far_rows = from_others(
        lax.ppermute(row_piece, "gx", Z_LO), "gx", X_NEXT, X_FAR, X_PREV
    )
    middles = from_others(
        jnp.concatenate([w_next, w_prev], axis=1), "gy", Y_NEXT, Y_FAR, Y_PREV
    )
    lasts = from_others(w_far, "gy", Y_NEXT, Y_FAR, Y_PREV)

    inner = lax.all_gather(
        jnp.concatenate([hidden_in, attend_in.T], axis=0), "gy", axis=0, tiled=False
    )

    pre_float = hidden_pre.astype(F32)
    slope = gelu_slope(pre_float).astype(BF16)
    activated = gelu_value(pre_float).astype(BF16)

    grads, normed_slab, turned = assemble(place, near_rows + far_rows)
    own_grads = grads[:, :384]

    merge_mine = merge_part(
        place, grads, [w for s in range(4) for w in (firsts[s], middles[s], lasts[s])]
    )
    merge_other = lax.ppermute(merge_mine, "gz", CORE)
    projected_grad = attend(projected, merge_mine, merge_other)

    hidden, inner_grads = [None] * 4, [None] * 4
    for step in (2, 1, 3, 0):
        mine = hidden_part(grads, firsts[step], middles[step], lasts[step])
        other = lax.ppermute(mine, "gz", CORE)
        hidden[step], inner_grads[step] = hidden_step(
            place, step, mine, other, slope, turned
        )

    part_attend_out = jnp.einsum("tg,td->gd", mixed_heads, own_grads, preferred_element_type=F32)
    part_hidden_out = jnp.einsum("tg,td->gd", activated, own_grads, preferred_element_type=F32)
    sum_attend_out = lax.psum_scatter(
        part_attend_out.astype(BF16), "gy", scatter_dimension=0, tiled=True
    )
    sum_hidden_out = lax.psum_scatter(
        part_hidden_out.astype(BF16), "gy", scatter_dimension=0, tiled=True
    )

    def over_y(chunks):
        got = [chunks[0]] + [
            lax.ppermute(chunks[step], "gy", perm)
            for step, perm in ((2, Y_FAR), (1, Y_PREV), (3, Y_NEXT))
        ]
        return sum(part.astype(F32) for part in got).astype(BF16)

    part_attend_in = jnp.einsum(
        "tq,td->qd", projected_grad, normed_slab, preferred_element_type=F32
    ).astype(BF16)
    sum_attend_in = over_y(
        [
            lax.dynamic_slice_in_dim(part_attend_in, (place[2] + step) % 4 * 288, 288, 0)
            for step in range(4)
        ]
    ).T
    sum_hidden_in = over_y(inner_grads)

    rows = input_part(place, projected_grad, inner, hidden)
    got = [rows[0]] + [
        lax.ppermute(rows[step], "gx", perm)
        for step, perm in ((2, X_FAR), (1, X_PREV), (3, X_NEXT))
    ]
    total = sum(part.astype(F32) for part in got)
    beyond = lax.ppermute(total[128:].astype(BF16), "gx", Z_LO)
    normed_grad = (total[:128] + beyond.astype(F32)).astype(BF16)
    return normed_grad, sum_attend_in, sum_hidden_in, sum_attend_out, sum_hidden_out


def solution(mesh):
    placed = (
        P(("gy", "gx"), "gz"),
        P(("gy", "gx"), "gz"),
        P("gy", "gx"),
        P("gy", "gx"),
        P("gy", "gx"),
        P("gz", ("gx", "gy")),
        P("gz", ("gx", "gy")),
        P(("gx", "gy"), "gz"),
        P(("gx", "gy"), "gz"),
    )
    return jax.shard_map(
        local,
        mesh=mesh,
        in_specs=placed,
        out_specs=(
            P(("gy", "gx"), "gz"),
            P("gz", ("gx", "gy")),
            P("gz", ("gx", "gy")),
            P(("gx", "gy"), "gz"),
            P(("gx", "gy"), "gz"),
        ),
        check_vma=False,
    )
```

```python
import functools

import jax
import jax.numpy as jnp
from jax import lax
from jax.experimental import pallas as pl
from jax.experimental.pallas import tpu as pltpu
from jax.sharding import PartitionSpec as P

HEAD = 128
F32 = jnp.float32
BF16 = jnp.bfloat16
NT = (((1,), (1,)), ((), ()))
NN = (((1,), (0,)), ((), ()))
VMEM_LIMIT = 24 * 1024 * 1024

X_NEXT = [(i, i // 4 * 4 + (i + 3) % 4) for i in range(8)]
X_FAR = [(i, i // 4 * 4 + (i + 2) % 4) for i in range(8)]
X_PREV = [(i, i // 4 * 4 + (i + 1) % 4) for i in range(8)]
Z_LO = [(i, (i + 4) % 8) for i in range(8)]
Y_NEXT = [(i, (i + 3) % 4) for i in range(4)]
Y_FAR = [(i, (i + 2) % 4) for i in range(4)]
Y_PREV = [(i, (i + 1) % 4) for i in range(4)]
Z_NEXT = [(i, (i + 6) % 8) for i in range(8)]
Z_FAR = [(i, (i + 4) % 8) for i in range(8)]
Z_PREV = [(i, (i + 2) % 8) for i in range(8)]
CORE = [(i, i ^ 1) for i in range(8)]


def gelu_value(values):
    return 0.5 * values * (1.0 + lax.erf(values * 0.7071067811865476))


def gelu_slope(values):
    return (
        0.5 * (1.0 + lax.erf(values * 0.7071067811865476))
        + values * jnp.exp(-0.5 * values * values) * 0.3989422804014327
    )


def dot(a, b, dims):
    return lax.dot_general(a, b, dims, preferred_element_type=F32)


def from_others(value, axis, nxt, far, prv):
    return [
        value,
        lax.ppermute(value, axis, nxt),
        lax.ppermute(value, axis, far),
        lax.ppermute(value, axis, prv),
    ]


def to_owners(chunks):
    return [
        chunks[0],
        lax.ppermute(chunks[2], "gy", Y_FAR),
        lax.ppermute(chunks[1], "gy", Y_PREV),
        lax.ppermute(chunks[3], "gy", Y_NEXT),
    ]


def added(parts):
    return sum(part.astype(F32) for part in parts).astype(BF16)


def whole(count):
    return [pl.BlockSpec(memory_space=pltpu.VMEM)] * count


def params():
    return pltpu.CompilerParams(vmem_limit_bytes=VMEM_LIMIT)


def cost(micros):
    return pl.CostEstimate(flops=int(micros * 0.1e9), bytes_accessed=0, transcendentals=0)


def spread_body(place, got_ref, inner_ref, rows_ref, heads_ref):
    for step in range(4):
        index = lax.rem(place[3] + step, 4)
        rows_ref[:, step * 384 : step * 384 + 384] = got_ref[index, :256, :]
        heads_ref[step * 96 : step * 96 + 96, :] = got_ref[index, 256:, :]
    heads_ref[384:, :] = inner_ref[...]


def spread(place, got, inner):
    return pl.pallas_call(
        spread_body,
        in_specs=[pl.BlockSpec(memory_space=pltpu.SMEM)] + whole(2),
        out_specs=whole(2),
        out_shape=(
            jax.ShapeDtypeStruct((256, 1536), BF16),
            jax.ShapeDtypeStruct((672, 384), BF16),
        ),
        compiler_params=params(),
        cost_estimate=cost(2),
        name="spread",
    )(place, got, inner)


def repeat_body(place, got_ref, out_ref):
    for step in range(1, 4):
        value = got_ref[lax.rem(place[3] + step, 4)]
        for copy in range(4):
            out_ref[copy, :, step * 384 - 384 : step * 384] = value


def repeat(place, got):
    return pl.pallas_call(
        repeat_body,
        in_specs=[pl.BlockSpec(memory_space=pltpu.SMEM)] + whole(1),
        out_specs=pl.BlockSpec(memory_space=pltpu.VMEM),
        out_shape=jax.ShapeDtypeStruct((4, 384, 1152), BF16),
        compiler_params=params(),
        cost_estimate=cost(2),
        name="repeat",
    )(place, got)


def block_of(place, step, side):
    index = lax.rem(place[1] + side, 2) * 4 + lax.rem(place[0] + step, 4)
    return pl.ds(pl.multiple_of(index * 128, 128), 128)


def assemble_body(place, own, after, before, far_a, far_b, grad_ref):
    for side, far in enumerate((far_a, far_b)):
        part = slice(side * 128, side * 128 + 128)
        grad_ref[block_of(place, 0, side), :] = own[part, :]
        grad_ref[block_of(place, 1, side), :] = after[part, :]
        grad_ref[block_of(place, 3, side), :] = before[part, :]
        grad_ref[block_of(place, 2, side), :] = far[...]


def assemble(place, pieces):
    return pl.pallas_call(
        assemble_body,
        in_specs=[pl.BlockSpec(memory_space=pltpu.SMEM)] + whole(5),
        out_specs=pl.BlockSpec(memory_space=pltpu.VMEM),
        out_shape=jax.ShapeDtypeStruct((1024, 1536), BF16),
        compiler_params=params(),
        cost_estimate=cost(2),
        name="assemble",
    )(place, *pieces)


def assemble_norm_body(place, *refs):
    pieces, norm_ref, turned_ref = refs[:4], refs[4], refs[5]
    for step in range(4):
        for side in range(2):
            at = block_of(place, step, side)
            rows = pieces[step][side * 128 : side * 128 + 128, :]
            norm_ref[at, :] = rows
            turned_ref[:, at] = rows.T


def assemble_norm(place, pieces):
    return pl.pallas_call(
        assemble_norm_body,
        in_specs=[pl.BlockSpec(memory_space=pltpu.SMEM)] + whole(4),
        out_specs=whole(2),
        out_shape=(
            jax.ShapeDtypeStruct((1024, 384), BF16),
            jax.ShapeDtypeStruct((384, 1024), BF16),
        ),
        compiler_params=params(),
        cost_estimate=cost(2),
        name="assemble_norm",
    )(place, *pieces)


def hidden_body(steps, place, grad_ref, *refs):
    firsts, lasts, out_ref, held = refs[:2], refs[2], refs[3], refs[4]

    @pl.when(pl.program_id(0) == 0)
    def _():
        for which, step in enumerate(steps):
            at = slice(which * 384, which * 384 + 384)
            held[at, :384] = firsts[which][...]
            held[at, 384:] = lasts[lax.rem(place[2] + step, 4)]

    out_ref[...] = dot(grad_ref[...], held[...], NT).astype(BF16)


def hidden_part(place, steps, grads, firsts, lasts):
    return pl.pallas_call(
        functools.partial(hidden_body, steps),
        grid=(2,),
        in_specs=[
            pl.BlockSpec(memory_space=pltpu.SMEM),
            pl.BlockSpec((512, 1536), lambda i: (i, 0)),
        ]
        + [pl.BlockSpec((384, 384), lambda i: (0, 0))] * 2
        + [pl.BlockSpec((4, 384, 1152), lambda i: (0, 0, 0))],
        out_specs=pl.BlockSpec((512, 768), lambda i: (i, 0)),
        out_shape=jax.ShapeDtypeStruct((1024, 768), BF16),
        scratch_shapes=[pltpu.VMEM((768, 1536), BF16)],
        compiler_params=params(),
        cost_estimate=cost(4),
        name="hidden_part",
    )(place, grads, firsts[steps[0]], firsts[steps[1]], lasts)


def merge_body(place, grad_ref, *refs):
    weights, out_ref, held = refs[:4], refs[4], refs[5]

    @pl.when(pl.program_id(0) == 0)
    def _():
        for step in range(4):
            row = lax.rem(place[2] + step, 4) * 96
            at = pl.ds(pl.multiple_of(row, 32), 96)
            for part in range(4):
                held[at, part * 384 : part * 384 + 384] = weights[step][
                    part * 96 : part * 96 + 96, :
                ]

    out_ref[...] = dot(grad_ref[...], held[...], NT).astype(BF16)


def merge_part(place, grads, weights):
    return pl.pallas_call(
        merge_body,
        grid=(2,),
        in_specs=[
            pl.BlockSpec(memory_space=pltpu.SMEM),
            pl.BlockSpec((512, 1536), lambda i: (i, 0)),
        ]
        + [pl.BlockSpec((384, 384), lambda i: (0, 0)) for w in weights],
        out_specs=pl.BlockSpec((512, 384), lambda i: (i, 0)),
        out_shape=jax.ShapeDtypeStruct((1024, 384), BF16),
        scratch_shapes=[pltpu.VMEM((384, 1536), BF16)],
        compiler_params=params(),
        cost_estimate=cost(3),
        name="merge_part",
    )(place, grads, *weights)


SPAN = 256


def attend_body(rows_ref, mine_ref, other_ref, out_ref, key_sum, value_sum):
    scale = HEAD ** (-0.5)
    power = scale * 1.4426950408889634
    keys = rows_ref[:, HEAD : 2 * HEAD]
    values = rows_ref[:, 2 * HEAD :]
    turned = keys.T
    for part in range(1024 // SPAN):
        at = slice(part * SPAN, (part + 1) * SPAN)
        queries = rows_ref[at, :HEAD]
        grads = (mine_ref[at, :].astype(F32) + other_ref[at, :].astype(F32)).astype(BF16)
        scores = dot(keys, queries, NT)
        largest = jnp.max(scores, axis=0, keepdims=True)
        weights = jnp.exp2((scores - largest) * power)
        inverse = 1.0 / jnp.sum(weights, axis=0, keepdims=True)
        probability = weights * inverse
        prob_grad = dot(values, grads, NT)
        centre = jnp.sum(probability * prob_grad, axis=0, keepdims=True)
        score_grad = (probability * (prob_grad - centre)).astype(BF16)
        key_part = dot(score_grad, queries, NN)
        value_part = dot(probability.astype(BF16), grads, NN)
        if part == 0:
            key_sum[...] = key_part
            value_sum[...] = value_part
        else:
            key_sum[...] += key_part
            value_sum[...] += value_part
        query_grad = dot(turned, score_grad, NN) * scale
        out_ref[at, :HEAD] = query_grad.T.astype(BF16)
    out_ref[:, HEAD : 2 * HEAD] = (key_sum[...] * scale).astype(BF16)
    out_ref[:, 2 * HEAD :] = value_sum[...].astype(BF16)


def attend(projected, mine, other):
    heads = projected.shape[1] // (3 * HEAD)
    return pl.pallas_call(
        attend_body,
        grid=(heads,),
        in_specs=[
            pl.BlockSpec((1024, 3 * HEAD), lambda h: (0, h)),
            pl.BlockSpec((1024, HEAD), lambda h: (0, h)),
            pl.BlockSpec((1024, HEAD), lambda h: (0, h)),
        ],
        out_specs=pl.BlockSpec((1024, 3 * HEAD), lambda h: (0, h)),
        out_shape=jax.ShapeDtypeStruct(projected.shape, BF16),
        scratch_shapes=[pltpu.VMEM((1024, HEAD), F32)] * 2,
        compiler_params=params(),
        cost_estimate=cost(16),
        name="attend",
    )(projected, mine, other)


def hidden_step_body(
    place, mine_ref, other_ref, slope_a, slope_b, turned_ref, grad_ref, out_a, out_b
):
    for slope_ref, out_ref, at in (
        (slope_a, out_a, slice(0, 384)),
        (slope_b, out_b, slice(384, 768)),
    ):
        total = mine_ref[:, at].astype(F32) + other_ref[:, at].astype(F32)
        grad = (total * slope_ref[...].astype(F32)).astype(BF16)
        grad_ref[:, at] = grad
        out_ref[...] = dot(turned_ref[...], grad, NN).astype(BF16)


def hidden_step(place, steps, mine, other, slope, turned):
    return pl.pallas_call(
        hidden_step_body,
        grid_spec=pltpu.PrefetchScalarGridSpec(
            num_scalar_prefetch=1,
            grid=(1,),
            in_specs=[
                pl.BlockSpec((1024, 768), lambda i, p: (0, 0)),
                pl.BlockSpec((1024, 768), lambda i, p: (0, 0)),
                pl.BlockSpec((1024, 384), lambda i, p: (0, lax.rem(p[2] + steps[0], 4))),
                pl.BlockSpec((1024, 384), lambda i, p: (0, lax.rem(p[2] + steps[1], 4))),
                pl.BlockSpec((384, 1024), lambda i, p: (0, 0)),
            ],
            out_specs=[
                pl.BlockSpec((1024, 768), lambda i, p: (0, 0)),
                pl.BlockSpec((384, 384), lambda i, p: (0, 0)),
                pl.BlockSpec((384, 384), lambda i, p: (0, 0)),
            ],
        ),
        out_shape=(
            jax.ShapeDtypeStruct((1024, 768), BF16),
            jax.ShapeDtypeStruct((384, 384), BF16),
            jax.ShapeDtypeStruct((384, 384), BF16),
        ),
        compiler_params=params(),
        cost_estimate=cost(4),
        name="hidden_step",
    )(place, mine, other, slope, slope, turned)


PAIRS = ((2, 1), (3, 0))


def input_body(place, *refs):
    attend_ref, turned, weights, hidden = refs[0], refs[1:5], refs[5:9], refs[9:11]
    out_ref, held = refs[11], refs[12]
    for step in range(4):
        row = lax.rem(place[2] + step, 4) * 288
        held[pl.ds(pl.multiple_of(row, 32), 288), :] = turned[step][384:, :]
    total = dot(attend_ref[...], held[...], NN)
    for which, steps in enumerate(PAIRS):
        for half, step in enumerate(steps):
            total += dot(
                hidden[which][:, half * 384 : half * 384 + 384],
                weights[step][384:, :],
                NT,
            )
    out_ref[...] = total.astype(BF16)


def input_part(place, projected_grad, turned, weights, hidden):
    return pl.pallas_call(
        input_body,
        in_specs=[pl.BlockSpec(memory_space=pltpu.SMEM)] + whole(11),
        out_specs=pl.BlockSpec(memory_space=pltpu.VMEM),
        out_shape=jax.ShapeDtypeStruct((1024, 384), BF16),
        scratch_shapes=[pltpu.VMEM((1152, 384), BF16)],
        compiler_params=params(),
        cost_estimate=cost(5),
        name="input_part",
    )(place, projected_grad, *turned, *weights, *hidden)


def local(
    normed,
    out_grad,
    projected,
    mixed_heads,
    hidden_pre,
    attend_in,
    hidden_in,
    attend_out,
    hidden_out,
):
    across = lax.axis_index("gx")
    place = jnp.stack(
        [across % 4, across // 4, lax.axis_index("gy"), lax.axis_index("gz") // 2]
    ).astype(jnp.int32)

    def over_z(value):
        return lax.all_to_all(
            jnp.broadcast_to(value[None], (4,) + value.shape),
            "gz",
            0,
            0,
            axis_index_groups=[[0, 2, 4, 6], [1, 3, 5, 7]],
        )

    own_rows = jnp.concatenate([out_grad, normed], axis=0)
    beyond = lax.ppermute(own_rows, "gx", Z_LO)
    small = jnp.concatenate([out_grad, beyond[:128], attend_out], axis=0)
    smalls = over_z(small)
    firsts = from_others(
        jnp.concatenate([hidden_out, hidden_in], axis=0), "gy", Y_NEXT, Y_FAR, Y_PREV
    )
    norms = from_others(
        jnp.concatenate([normed, beyond[128:]], axis=0), "gx", X_NEXT, X_FAR, X_PREV
    )
    pre_float = hidden_pre.astype(F32)
    slope = gelu_slope(pre_float).astype(BF16)
    activated = gelu_value(pre_float).astype(BF16)
    smalls, firsts, weights, norms, slope, activated = lax.optimization_barrier(
        (smalls, firsts, hidden_out, norms, slope, activated)
    )
    row_piece, head_piece = spread(place, smalls, attend_in.T)

    after = lax.ppermute(row_piece, "gx", X_NEXT)
    before = lax.ppermute(row_piece, "gx", X_PREV)
    rows = [
        row_piece,
        after,
        before,
        lax.ppermute(before[:128], "gx", X_PREV),
        lax.ppermute(after[128:], "gx", X_NEXT),
    ]

    others_z = repeat(place, over_z(weights))
    head_weights = from_others(head_piece, "gy", Y_NEXT, Y_FAR, Y_PREV)
    others_z, head_weights, rows = lax.optimization_barrier(
        (others_z, head_weights, rows)
    )
    lasts = lax.all_to_all(others_z, "gy", 0, 0)

    grads = assemble(place, rows)
    normed_slab, turned = assemble_norm(place, norms)
    own_grads = grads[:, :384]
    merge_mine = merge_part(place, grads, head_weights)
    merge_other = lax.ppermute(merge_mine, "gz", CORE)
    projected_grad = attend(projected, merge_mine, merge_other)
    parts = (
        jnp.einsum("tg,td->gd", activated, own_grads, preferred_element_type=F32),
        jnp.einsum("tg,td->gd", mixed_heads, own_grads, preferred_element_type=F32),
        jnp.einsum("tq,td->qd", projected_grad, normed_slab, preferred_element_type=F32),
    )
    chunks = [
        jnp.concatenate(
            [
                lax.dynamic_slice_in_dim(
                    part.astype(BF16), (place[2] + step) % 4 * size, size, 0
                )
                for part, size in zip(parts, (384, 96, 288), strict=True)
            ],
            axis=0,
        )
        for step in range(4)
    ]
    lasts, chunks = lax.optimization_barrier((lasts, chunks))

    got = to_owners(chunks)
    mines = [hidden_part(place, steps, grads, firsts, lasts) for steps in PAIRS]
    others = [lax.ppermute(mine, "gz", CORE) for mine in mines]
    hidden, inner_grads = [], [None] * 4
    for which, steps in enumerate(PAIRS):
        grad, inner_grads[steps[0]], inner_grads[steps[1]] = hidden_step(
            place, steps, mines[which], others[which], slope, turned
        )
        hidden.append(grad)
    inner_got = to_owners(inner_grads)

    rows = input_part(place, projected_grad, head_weights, firsts, hidden)
    rows = lax.all_to_all(rows.reshape(8, 128, 384), "gx", 0, 0)
    normed_grad = jnp.sum(rows.astype(F32), axis=0).astype(BF16)
    sums = added(got)
    return normed_grad, sums[480:].T, added(inner_got), sums[384:480], sums[:384]


def solution(mesh):
    placed = (
        P(("gy", "gx"), "gz"),
        P(("gy", "gx"), "gz"),
        P("gy", "gx"),
        P("gy", "gx"),
        P("gy", "gx"),
        P("gz", ("gx", "gy")),
        P("gz", ("gx", "gy")),
        P(("gx", "gy"), "gz"),
        P(("gx", "gy"), "gz"),
    )
    return jax.shard_map(
        local,
        mesh=mesh,
        in_specs=placed,
        out_specs=(
            P(("gy", "gx"), "gz"),
            P("gz", ("gx", "gy")),
            P("gz", ("gx", "gy")),
            P(("gx", "gy"), "gz"),
            P(("gx", "gy"), "gz"),
        ),
        check_vma=False,
    )
```

```python
import functools

import jax
import jax.numpy as jnp
from jax import lax
from jax.experimental import pallas as pl
from jax.experimental.pallas import tpu as pltpu
from jax.sharding import PartitionSpec as P

HEAD = 128
F32 = jnp.float32
BF16 = jnp.bfloat16
NT = (((1,), (1,)), ((), ()))
NN = (((1,), (0,)), ((), ()))
VMEM_LIMIT = 24 * 1024 * 1024

X_NEXT = [(i, i // 4 * 4 + (i + 3) % 4) for i in range(8)]
X_FAR = [(i, i // 4 * 4 + (i + 2) % 4) for i in range(8)]
X_PREV = [(i, i // 4 * 4 + (i + 1) % 4) for i in range(8)]
Z_LO = [(i, (i + 4) % 8) for i in range(8)]
Y_NEXT = [(i, (i + 3) % 4) for i in range(4)]
Y_FAR = [(i, (i + 2) % 4) for i in range(4)]
Y_PREV = [(i, (i + 1) % 4) for i in range(4)]
Z_NEXT = [(i, (i + 6) % 8) for i in range(8)]
Z_FAR = [(i, (i + 4) % 8) for i in range(8)]
Z_PREV = [(i, (i + 2) % 8) for i in range(8)]
CORE = [(i, i ^ 1) for i in range(8)]


def gelu_value(values):
    return 0.5 * values * (1.0 + lax.erf(values * 0.7071067811865476))


def gelu_slope(values):
    return (
        0.5 * (1.0 + lax.erf(values * 0.7071067811865476))
        + values * jnp.exp(-0.5 * values * values) * 0.3989422804014327
    )


def dot(a, b, dims):
    return lax.dot_general(a, b, dims, preferred_element_type=F32)


def from_others(value, axis, nxt, far, prv):
    return [
        value,
        lax.ppermute(value, axis, nxt),
        lax.ppermute(value, axis, far),
        lax.ppermute(value, axis, prv),
    ]


def to_owners(chunks):
    return [
        chunks[0],
        lax.ppermute(chunks[2], "gy", Y_FAR),
        lax.ppermute(chunks[1], "gy", Y_PREV),
        lax.ppermute(chunks[3], "gy", Y_NEXT),
    ]


def added(parts):
    return sum(part.astype(F32) for part in parts).astype(BF16)


def whole(count):
    return [pl.BlockSpec(memory_space=pltpu.VMEM)] * count


def params():
    return pltpu.CompilerParams(vmem_limit_bytes=VMEM_LIMIT)


def cost(micros):
    return pl.CostEstimate(flops=int(micros * 0.01e9), bytes_accessed=0, transcendentals=0)


def spread_body(place, got_ref, inner_ref, rows_ref, heads_ref):
    for step in range(4):
        index = lax.rem(place[3] + step, 4)
        rows_ref[:, step * 384 : step * 384 + 384] = got_ref[index, :256, :]
        heads_ref[step * 96 : step * 96 + 96, :] = got_ref[index, 256:, :]
    heads_ref[384:, :] = inner_ref[...]


def spread(place, got, inner):
    return pl.pallas_call(
        spread_body,
        in_specs=[pl.BlockSpec(memory_space=pltpu.SMEM)] + whole(2),
        out_specs=whole(2),
        out_shape=(
            jax.ShapeDtypeStruct((256, 1536), BF16),
            jax.ShapeDtypeStruct((768, 384), BF16),
        ),
        compiler_params=params(),
        cost_estimate=cost(2),
        name="spread",
    )(place, got, inner)


def others_body(place, got_ref, out_ref):
    for step in range(1, 4):
        value = got_ref[lax.rem(place[3] + step, 4)]
        out_ref[:, step * 384 - 384 : step * 384] = value


def others_of(place, got):
    return pl.pallas_call(
        others_body,
        in_specs=[pl.BlockSpec(memory_space=pltpu.SMEM)] + whole(1),
        out_specs=pl.BlockSpec(memory_space=pltpu.VMEM),
        out_shape=jax.ShapeDtypeStruct((384, 1152), BF16),
        compiler_params=params(),
        cost_estimate=cost(1),
        name="others_of",
    )(place, got)


def block_of(place, step, side):
    index = lax.rem(place[1] + side, 2) * 4 + lax.rem(place[0] + step, 4)
    return pl.ds(pl.multiple_of(index * 128, 128), 128)


def assemble_body(place, own, after, before, far_a, far_b, grad_ref):
    for side, far in enumerate((far_a, far_b)):
        part = slice(side * 128, side * 128 + 128)
        grad_ref[block_of(place, 0, side), :] = own[part, :]
        grad_ref[block_of(place, 1, side), :] = after[part, :]
        grad_ref[block_of(place, 3, side), :] = before[part, :]
        grad_ref[block_of(place, 2, side), :] = far[...]


def assemble(place, pieces):
    return pl.pallas_call(
        assemble_body,
        in_specs=[pl.BlockSpec(memory_space=pltpu.SMEM)] + whole(5),
        out_specs=pl.BlockSpec(memory_space=pltpu.VMEM),
        out_shape=jax.ShapeDtypeStruct((1024, 1536), BF16),
        compiler_params=params(),
        cost_estimate=cost(2),
        name="assemble",
    )(place, *pieces)


def assemble_norm_body(place, *refs):
    pieces, norm_ref, turned_ref = refs[:4], refs[4], refs[5]
    for step in range(4):
        for side in range(2):
            at = block_of(place, step, side)
            rows = pieces[step][side * 128 : side * 128 + 128, :]
            norm_ref[at, :] = rows
            turned_ref[:, at] = rows.T


def assemble_norm(place, pieces):
    return pl.pallas_call(
        assemble_norm_body,
        in_specs=[pl.BlockSpec(memory_space=pltpu.SMEM)] + whole(4),
        out_specs=whole(2),
        out_shape=(
            jax.ShapeDtypeStruct((1024, 384), BF16),
            jax.ShapeDtypeStruct((384, 1024), BF16),
        ),
        compiler_params=params(),
        cost_estimate=cost(2),
        name="assemble_norm",
    )(place, *pieces)


def hidden_body(grad_ref, *refs):
    firsts, lasts, out_ref, held = refs[:2], refs[2:-2], refs[-2], refs[-1]

    @pl.when(pl.program_id(0) == 0)
    def _():
        for which in range(2):
            held[which * 384 : which * 384 + 384, :384] = firsts[which][...]
        row = 0
        for last in lasts:
            held[row : row + last.shape[0], 384:] = last[...]
            row += last.shape[0]

    out_ref[...] = dot(grad_ref[...], held[...], NT).astype(BF16)


def hidden_part(grads, firsts, lasts):
    return pl.pallas_call(
        hidden_body,
        grid=(2,),
        in_specs=[pl.BlockSpec((512, 1536), lambda i: (i, 0))]
        + [pl.BlockSpec((384, 384), lambda i: (0, 0))] * 2
        + [pl.BlockSpec(last.shape, lambda i: (0, 0)) for last in lasts],
        out_specs=pl.BlockSpec((512, 768), lambda i: (i, 0)),
        out_shape=jax.ShapeDtypeStruct((1024, 768), BF16),
        scratch_shapes=[pltpu.VMEM((768, 1536), BF16)],
        compiler_params=params(),
        cost_estimate=cost(4),
        name="hidden_part",
    )(grads, *firsts, *lasts)


def merge_body(place, grad_ref, *refs):
    weights, out_ref, held = refs[:4], refs[4], refs[5]

    @pl.when(pl.program_id(0) == 0)
    def _():
        for step in range(4):
            row = lax.rem(place[2] + step, 4) * 96
            at = pl.ds(pl.multiple_of(row, 32), 96)
            for part in range(4):
                held[at, part * 384 : part * 384 + 384] = weights[step][
                    part * 96 : part * 96 + 96, :
                ]

    out_ref[...] = dot(grad_ref[...], held[...], NT).astype(BF16)


def merge_part(place, grads, weights):
    return pl.pallas_call(
        merge_body,
        grid=(2,),
        in_specs=[
            pl.BlockSpec(memory_space=pltpu.SMEM),
            pl.BlockSpec((512, 1536), lambda i: (i, 0)),
        ]
        + [pl.BlockSpec((384, 384), lambda i: (0, 0)) for w in weights],
        out_specs=pl.BlockSpec((512, 384), lambda i: (i, 0)),
        out_shape=jax.ShapeDtypeStruct((1024, 384), BF16),
        scratch_shapes=[pltpu.VMEM((384, 1536), BF16)],
        compiler_params=params(),
        cost_estimate=cost(3),
        name="merge_part",
    )(place, grads, *weights)


SPAN = 256


def attend_body(rows_ref, mine_ref, other_ref, out_ref, key_sum, value_sum):
    scale = HEAD ** (-0.5)
    power = scale * 1.4426950408889634
    keys = rows_ref[:, HEAD : 2 * HEAD]
    values = rows_ref[:, 2 * HEAD :]
    turned = keys.T
    for part in range(1024 // SPAN):
        at = slice(part * SPAN, (part + 1) * SPAN)
        queries = rows_ref[at, :HEAD]
        grads = (mine_ref[at, :].astype(F32) + other_ref[at, :].astype(F32)).astype(BF16)
        scores = dot(keys, queries, NT)
        largest = jnp.max(scores, axis=0, keepdims=True)
        weights = jnp.exp2((scores - largest) * power)
        inverse = 1.0 / jnp.sum(weights, axis=0, keepdims=True)
        probability = weights * inverse
        prob_grad = dot(values, grads, NT)
        centre = jnp.sum(probability * prob_grad, axis=0, keepdims=True)
        score_grad = (probability * (prob_grad - centre)).astype(BF16)
        key_part = dot(score_grad, queries, NN)
        value_part = dot(probability.astype(BF16), grads, NN)
        if part == 0:
            key_sum[...] = key_part
            value_sum[...] = value_part
        else:
            key_sum[...] += key_part
            value_sum[...] += value_part
        query_grad = dot(turned, score_grad, NN) * scale
        out_ref[at, :HEAD] = query_grad.T.astype(BF16)
    out_ref[:, HEAD : 2 * HEAD] = (key_sum[...] * scale).astype(BF16)
    out_ref[:, 2 * HEAD :] = value_sum[...].astype(BF16)


def attend(projected, mine, other, first, count, before=None):
    def body(*refs):
        attend_body(*refs[:3], *refs[-3:])

    def block(width):
        return pl.BlockSpec((1024, width), lambda h: (0, h + first))

    more = [] if before is None else [before]
    return pl.pallas_call(
        body,
        grid=(count,),
        in_specs=[block(3 * HEAD), block(HEAD), block(HEAD)]
        + [pl.BlockSpec(memory_space=pl.ANY)] * len(more),
        out_specs=block(3 * HEAD),
        out_shape=jax.ShapeDtypeStruct(projected.shape, BF16),
        input_output_aliases={3: 0} if more else {},
        scratch_shapes=[pltpu.VMEM((1024, HEAD), F32)] * 2,
        compiler_params=params(),
        cost_estimate=cost(5 * count),
        name="attend",
    )(projected, mine, other, *more)


def hidden_step_body(
    place, mine_ref, other_ref, slope_a, slope_b, turned_ref, grad_ref, out_a, out_b
):
    for slope_ref, out_ref, at in (
        (slope_a, out_a, slice(0, 384)),
        (slope_b, out_b, slice(384, 768)),
    ):
        total = mine_ref[:, at].astype(F32) + other_ref[:, at].astype(F32)
        grad = (total * slope_ref[...].astype(F32)).astype(BF16)
        grad_ref[:, at] = grad
        out_ref[...] = dot(turned_ref[...], grad, NN).astype(BF16)


def hidden_step(place, steps, mine, other, slope, turned):
    return pl.pallas_call(
        hidden_step_body,
        grid_spec=pltpu.PrefetchScalarGridSpec(
            num_scalar_prefetch=1,
            grid=(1,),
            in_specs=[
                pl.BlockSpec((1024, 768), lambda i, p: (0, 0)),
                pl.BlockSpec((1024, 768), lambda i, p: (0, 0)),
                pl.BlockSpec((1024, 384), lambda i, p: (0, lax.rem(p[2] + steps[0], 4))),
                pl.BlockSpec((1024, 384), lambda i, p: (0, lax.rem(p[2] + steps[1], 4))),
                pl.BlockSpec((384, 1024), lambda i, p: (0, 0)),
            ],
            out_specs=[
                pl.BlockSpec((1024, 768), lambda i, p: (0, 0)),
                pl.BlockSpec((384, 384), lambda i, p: (0, 0)),
                pl.BlockSpec((384, 384), lambda i, p: (0, 0)),
            ],
        ),
        out_shape=(
            jax.ShapeDtypeStruct((1024, 768), BF16),
            jax.ShapeDtypeStruct((384, 384), BF16),
            jax.ShapeDtypeStruct((384, 384), BF16),
        ),
        compiler_params=params(),
        cost_estimate=cost(4),
        name="hidden_step",
    )(place, mine, other, slope, slope, turned)


CUT = (384, 96, 288)


def pack_body(place, hidden_ref, merge_ref, attend_ref, *outs):
    for step in range(4):
        owner, row = lax.rem(place[2] + step, 4), 0
        for ref, size in zip((hidden_ref, merge_ref, attend_ref), CUT, strict=True):
            at = pl.ds(pl.multiple_of(owner * size, 32), size)
            outs[step][row : row + size, :] = ref[at, :]
            row += size


def pack(place, parts):
    return pl.pallas_call(
        pack_body,
        in_specs=[pl.BlockSpec(memory_space=pltpu.SMEM)] + whole(3),
        out_specs=whole(4),
        out_shape=[jax.ShapeDtypeStruct((sum(CUT), 384), BF16)] * 4,
        compiler_params=params(),
        cost_estimate=cost(1),
        name="pack",
    )(place, *parts)


PAIRS = ((2, 1), (3, 0))


def input_body(place, *refs):
    attend_ref, turned, weights, hidden = refs[0], refs[1:5], refs[5:9], refs[9:11]
    out_ref, held = refs[11], refs[12]
    for step in range(4):
        row = lax.rem(place[2] + step, 4) * 288
        held[pl.ds(pl.multiple_of(row, 32), 288), :] = turned[step][384:, :]
    total = dot(attend_ref[...], held[...], NN)
    for which, steps in enumerate(PAIRS):
        for half, step in enumerate(steps):
            total += dot(
                hidden[which][:, half * 384 : half * 384 + 384],
                weights[step][384:, :],
                NT,
            )
    out_ref[...] = total.astype(BF16)


def input_part(place, projected_grad, turned, weights, hidden):
    return pl.pallas_call(
        input_body,
        in_specs=[pl.BlockSpec(memory_space=pltpu.SMEM)] + whole(11),
        out_specs=pl.BlockSpec(memory_space=pltpu.VMEM),
        out_shape=jax.ShapeDtypeStruct((1024, 384), BF16),
        scratch_shapes=[pltpu.VMEM((1152, 384), BF16)],
        compiler_params=params(),
        cost_estimate=cost(5),
        name="input_part",
    )(place, projected_grad, *turned, *weights, *hidden)


def local(
    normed,
    out_grad,
    projected,
    mixed_heads,
    hidden_pre,
    attend_in,
    hidden_in,
    attend_out,
    hidden_out,
):
    across = lax.axis_index("gx")
    place = jnp.stack(
        [across % 4, across // 4, lax.axis_index("gy"), lax.axis_index("gz") // 2]
    ).astype(jnp.int32)

    def over_z(value):
        return lax.all_to_all(
            jnp.broadcast_to(value[None], (4,) + value.shape),
            "gz",
            0,
            0,
            axis_index_groups=[[0, 2, 4, 6], [1, 3, 5, 7]],
        )

    own_rows = jnp.concatenate([out_grad, normed], axis=0)
    beyond = lax.ppermute(own_rows, "gx", Z_LO)
    small = jnp.concatenate([out_grad, beyond[:128], attend_out], axis=0)
    smalls = over_z(small)
    firsts = from_others(
        jnp.concatenate([hidden_out, attend_in.T], axis=0), "gy", Y_NEXT, Y_FAR, Y_PREV
    )
    norms = from_others(
        jnp.concatenate([normed, beyond[128:]], axis=0), "gx", X_NEXT, X_FAR, X_PREV
    )
    pre_float = hidden_pre.astype(F32)
    slope = gelu_slope(pre_float).astype(BF16)
    activated = gelu_value(pre_float).astype(BF16)
    smalls, weights, firsts, norms, slope, activated = lax.optimization_barrier(
        (smalls, hidden_out, firsts, norms, slope, activated)
    )
    row_piece, head_piece = spread(place, smalls, hidden_in)

    after = lax.ppermute(row_piece, "gx", X_NEXT)
    before = lax.ppermute(row_piece, "gx", X_PREV)
    rows = [
        row_piece,
        after,
        before,
        lax.ppermute(before[:128], "gx", X_PREV),
        lax.ppermute(after[128:], "gx", X_NEXT),
    ]

    others_z = others_of(place, over_z(weights))
    head_weights = from_others(head_piece, "gy", Y_NEXT, Y_FAR, Y_PREV)
    others_z, head_weights, rows = lax.optimization_barrier(
        (others_z, head_weights, rows)
    )
    last_after = lax.ppermute(others_z, "gy", Y_NEXT)
    last_before = lax.ppermute(others_z, "gy", Y_PREV)

    grads = assemble(place, rows)
    normed_slab, turned = assemble_norm(place, norms)
    own_grads = grads[:, :384]
    merge_mine = merge_part(place, grads, head_weights)
    merge_other = lax.ppermute(merge_mine, "gz", CORE)
    projected_grad = attend(projected, merge_mine, merge_other, 0, 2)
    projected_grad, last_after, last_before = lax.optimization_barrier(
        (projected_grad, last_after, last_before)
    )
    last_far = [
        lax.ppermute(last_before[:192], "gy", Y_PREV),
        lax.ppermute(last_after[192:], "gy", Y_NEXT),
    ]
    projected_grad = attend(projected, merge_mine, merge_other, 2, 1, projected_grad)
    parts = (
        jnp.einsum("tg,td->gd", activated, own_grads, preferred_element_type=F32),
        jnp.einsum("tg,td->gd", mixed_heads, own_grads, preferred_element_type=F32),
        jnp.einsum("tq,td->qd", projected_grad, normed_slab, preferred_element_type=F32),
    )
    chunks = pack(place, [part.astype(BF16) for part in parts])
    last_far, chunks = lax.optimization_barrier((last_far, chunks))

    got = to_owners(chunks)
    mines = [
        hidden_part(grads, [firsts[2], firsts[1]], last_far + [last_after]),
        hidden_part(grads, [firsts[3], firsts[0]], [last_before, others_z]),
    ]
    others = [lax.ppermute(mine, "gz", CORE) for mine in mines]
    hidden, inner_grads = [], [None] * 4
    for which, steps in enumerate(PAIRS):
        grad, inner_grads[steps[0]], inner_grads[steps[1]] = hidden_step(
            place, steps, mines[which], others[which], slope, turned
        )
        hidden.append(grad)
    inner_got = to_owners(inner_grads)

    rows = input_part(place, projected_grad, firsts, head_weights, hidden)
    rows = lax.all_to_all(rows.reshape(8, 128, 384), "gx", 0, 0)
    normed_grad = jnp.sum(rows.astype(F32), axis=0).astype(BF16)
    sums = added(got)
    return normed_grad, sums[480:].T, added(inner_got), sums[384:480], sums[:384]


def solution(mesh):
    placed = (
        P(("gy", "gx"), "gz"),
        P(("gy", "gx"), "gz"),
        P("gy", "gx"),
        P("gy", "gx"),
        P("gy", "gx"),
        P("gz", ("gx", "gy")),
        P("gz", ("gx", "gy")),
        P(("gx", "gy"), "gz"),
        P(("gx", "gy"), "gz"),
    )
    return jax.shard_map(
        local,
        mesh=mesh,
        in_specs=placed,
        out_specs=(
            P(("gy", "gx"), "gz"),
            P("gz", ("gx", "gy")),
            P("gz", ("gx", "gy")),
            P(("gx", "gy"), "gz"),
            P(("gx", "gy"), "gz"),
        ),
        check_vma=False,
    )
```

```python
import functools

import jax
import jax.numpy as jnp
from jax import lax
from jax.experimental import pallas as pl
from jax.experimental.pallas import tpu as pltpu
from jax.sharding import PartitionSpec as P

HEAD = 128
F32 = jnp.float32
BF16 = jnp.bfloat16
NT = (((1,), (1,)), ((), ()))
NN = (((1,), (0,)), ((), ()))
VMEM_LIMIT = 24 * 1024 * 1024

X_NEXT = [(i, i // 4 * 4 + (i + 3) % 4) for i in range(8)]
X_FAR = [(i, i // 4 * 4 + (i + 2) % 4) for i in range(8)]
X_PREV = [(i, i // 4 * 4 + (i + 1) % 4) for i in range(8)]
Z_LO = [(i, (i + 4) % 8) for i in range(8)]
Y_NEXT = [(i, (i + 3) % 4) for i in range(4)]
Y_FAR = [(i, (i + 2) % 4) for i in range(4)]
Y_PREV = [(i, (i + 1) % 4) for i in range(4)]
Z_NEXT = [(i, (i + 6) % 8) for i in range(8)]
Z_FAR = [(i, (i + 4) % 8) for i in range(8)]
Z_PREV = [(i, (i + 2) % 8) for i in range(8)]
CORE = [(i, i ^ 1) for i in range(8)]


def gelu_value(values):
    return 0.5 * values * (1.0 + lax.erf(values * 0.7071067811865476))


def gelu_slope(values):
    return (
        0.5 * (1.0 + lax.erf(values * 0.7071067811865476))
        + values * jnp.exp(-0.5 * values * values) * 0.3989422804014327
    )


def dot(a, b, dims):
    return lax.dot_general(a, b, dims, preferred_element_type=F32)


def from_others(value, axis, nxt, far, prv):
    return [
        value,
        lax.ppermute(value, axis, nxt),
        lax.ppermute(value, axis, far),
        lax.ppermute(value, axis, prv),
    ]


def to_owners(chunks):
    return [
        chunks[0],
        lax.ppermute(chunks[2], "gy", Y_FAR),
        lax.ppermute(chunks[1], "gy", Y_PREV),
        lax.ppermute(chunks[3], "gy", Y_NEXT),
    ]


def added(parts):
    return sum(part.astype(F32) for part in parts).astype(BF16)


def whole(count):
    return [pl.BlockSpec(memory_space=pltpu.VMEM)] * count


def params():
    return pltpu.CompilerParams(vmem_limit_bytes=VMEM_LIMIT)


def cost(micros):
    return pl.CostEstimate(flops=int(micros * 0.01e9), bytes_accessed=0, transcendentals=0)


def spread_body(place, got_ref, inner_ref, rows_ref, heads_ref):
    for step in range(4):
        index = lax.rem(place[3] + step, 4)
        rows_ref[:, step * 384 : step * 384 + 384] = got_ref[index, :256, :]
        heads_ref[step * 96 : step * 96 + 96, :] = got_ref[index, 256:, :]
    heads_ref[384:, :] = inner_ref[...]


def spread(place, got, inner):
    return pl.pallas_call(
        spread_body,
        in_specs=[pl.BlockSpec(memory_space=pltpu.SMEM)] + whole(2),
        out_specs=whole(2),
        out_shape=(
            jax.ShapeDtypeStruct((256, 1536), BF16),
            jax.ShapeDtypeStruct((768, 384), BF16),
        ),
        compiler_params=params(),
        cost_estimate=cost(2),
        name="spread",
    )(place, got, inner)


def others_body(place, got_ref, out_ref):
    for step in range(1, 4):
        value = got_ref[lax.rem(place[3] + step, 4)]
        out_ref[:, step * 384 - 384 : step * 384] = value


def others_of(place, got):
    return pl.pallas_call(
        others_body,
        in_specs=[pl.BlockSpec(memory_space=pltpu.SMEM)] + whole(1),
        out_specs=pl.BlockSpec(memory_space=pltpu.VMEM),
        out_shape=jax.ShapeDtypeStruct((384, 1152), BF16),
        compiler_params=params(),
        cost_estimate=cost(1),
        name="others_of",
    )(place, got)


def block_of(place, step, side):
    index = lax.rem(place[1] + side, 2) * 4 + lax.rem(place[0] + step, 4)
    return pl.ds(pl.multiple_of(index * 128, 128), 128)


def assemble_body(place, own, after, before, far_a, far_b, grad_ref):
    for side, far in enumerate((far_a, far_b)):
        part = slice(side * 128, side * 128 + 128)
        grad_ref[block_of(place, 0, side), :] = own[part, :]
        grad_ref[block_of(place, 1, side), :] = after[part, :]
        grad_ref[block_of(place, 3, side), :] = before[part, :]
        grad_ref[block_of(place, 2, side), :] = far[...]


def assemble(place, pieces):
    return pl.pallas_call(
        assemble_body,
        in_specs=[pl.BlockSpec(memory_space=pltpu.SMEM)] + whole(5),
        out_specs=pl.BlockSpec(memory_space=pltpu.VMEM),
        out_shape=jax.ShapeDtypeStruct((1024, 1536), BF16),
        compiler_params=params(),
        cost_estimate=cost(2),
        name="assemble",
    )(place, *pieces)


def assemble_norm_body(place, *refs):
    pieces, norm_ref, turned_ref = refs[:4], refs[4], refs[5]
    for step in range(4):
        for side in range(2):
            at = block_of(place, step, side)
            rows = pieces[step][side * 128 : side * 128 + 128, :]
            norm_ref[at, :] = rows
            turned_ref[:, at] = rows.T


def assemble_norm(place, pieces):
    return pl.pallas_call(
        assemble_norm_body,
        in_specs=[pl.BlockSpec(memory_space=pltpu.SMEM)] + whole(4),
        out_specs=whole(2),
        out_shape=(
            jax.ShapeDtypeStruct((1024, 384), BF16),
            jax.ShapeDtypeStruct((384, 1024), BF16),
        ),
        compiler_params=params(),
        cost_estimate=cost(2),
        name="assemble_norm",
    )(place, *pieces)


def hidden_body(grad_ref, *refs):
    firsts, lasts, out_ref, held = refs[:2], refs[2:-2], refs[-2], refs[-1]

    @pl.when(pl.program_id(0) == 0)
    def _():
        for which in range(2):
            held[which * 384 : which * 384 + 384, :384] = firsts[which][...]
        row = 0
        for last in lasts:
            held[row : row + last.shape[0], 384:] = last[...]
            row += last.shape[0]

    out_ref[...] = dot(grad_ref[...], held[...], NT).astype(BF16)


def hidden_part(grads, firsts, lasts):
    return pl.pallas_call(
        hidden_body,
        grid=(2,),
        in_specs=[pl.BlockSpec((512, 1536), lambda i: (i, 0))]
        + [pl.BlockSpec((384, 384), lambda i: (0, 0))] * 2
        + [pl.BlockSpec(last.shape, lambda i: (0, 0)) for last in lasts],
        out_specs=pl.BlockSpec((512, 768), lambda i: (i, 0)),
        out_shape=jax.ShapeDtypeStruct((1024, 768), BF16),
        scratch_shapes=[pltpu.VMEM((768, 1536), BF16)],
        compiler_params=params(),
        cost_estimate=cost(4),
        name="hidden_part",
    )(grads, *firsts, *lasts)


def merge_body(place, grad_ref, *refs):
    weights, out_ref, held = refs[:4], refs[4], refs[5]

    @pl.when(pl.program_id(0) == 0)
    def _():
        for step in range(4):
            row = lax.rem(place[2] + step, 4) * 96
            at = pl.ds(pl.multiple_of(row, 32), 96)
            for part in range(4):
                held[at, part * 384 : part * 384 + 384] = weights[step][
                    part * 96 : part * 96 + 96, :
                ]

    out_ref[...] = dot(grad_ref[...], held[...], NT).astype(BF16)


def merge_part(place, grads, weights):
    return pl.pallas_call(
        merge_body,
        grid=(2,),
        in_specs=[
            pl.BlockSpec(memory_space=pltpu.SMEM),
            pl.BlockSpec((512, 1536), lambda i: (i, 0)),
        ]
        + [pl.BlockSpec((384, 384), lambda i: (0, 0)) for w in weights],
        out_specs=pl.BlockSpec((512, 384), lambda i: (i, 0)),
        out_shape=jax.ShapeDtypeStruct((1024, 384), BF16),
        scratch_shapes=[pltpu.VMEM((384, 1536), BF16)],
        compiler_params=params(),
        cost_estimate=cost(3),
        name="merge_part",
    )(place, grads, *weights)


SPAN = 256


def probability_body(rows_ref, out_ref):
    power = HEAD ** (-0.5) * 1.4426950408889634
    keys = rows_ref[:, HEAD : 2 * HEAD]
    for part in range(1024 // SPAN):
        at = slice(part * SPAN, (part + 1) * SPAN)
        scores = dot(keys, rows_ref[at, :HEAD], NT)
        largest = jnp.max(scores, axis=0, keepdims=True)
        weights = jnp.exp2((scores - largest) * power)
        inverse = 1.0 / jnp.sum(weights, axis=0, keepdims=True)
        out_ref[:, at] = (weights * inverse).astype(BF16)


def probabilities(projected):
    heads = projected.shape[1] // (3 * HEAD)
    return pl.pallas_call(
        probability_body,
        grid=(heads,),
        in_specs=[pl.BlockSpec((1024, 3 * HEAD), lambda h: (0, h))],
        out_specs=pl.BlockSpec((1024, 1024), lambda h: (0, h)),
        out_shape=jax.ShapeDtypeStruct((1024, heads * 1024), BF16),
        compiler_params=params(),
        cost_estimate=cost(6),
        name="probability",
    )(projected)


def attend_body(rows_ref, chance_ref, mine_ref, other_ref, out_ref, key_sum, value_sum):
    scale = HEAD ** (-0.5)
    keys = rows_ref[:, HEAD : 2 * HEAD]
    values = rows_ref[:, 2 * HEAD :]
    turned = keys.T
    for part in range(1024 // SPAN):
        at = slice(part * SPAN, (part + 1) * SPAN)
        queries = rows_ref[at, :HEAD]
        grads = (mine_ref[at, :].astype(F32) + other_ref[at, :].astype(F32)).astype(BF16)
        rounded = chance_ref[:, at]
        probability = rounded.astype(F32)
        prob_grad = dot(values, grads, NT)
        centre = jnp.sum(probability * prob_grad, axis=0, keepdims=True)
        score_grad = (probability * (prob_grad - centre)).astype(BF16)
        key_part = dot(score_grad, queries, NN)
        value_part = dot(rounded, grads, NN)
        if part == 0:
            key_sum[...] = key_part
            value_sum[...] = value_part
        else:
            key_sum[...] += key_part
            value_sum[...] += value_part
        query_grad = dot(turned, score_grad, NN) * scale
        out_ref[at, :HEAD] = query_grad.T.astype(BF16)
    out_ref[:, HEAD : 2 * HEAD] = (key_sum[...] * scale).astype(BF16)
    out_ref[:, 2 * HEAD :] = value_sum[...].astype(BF16)


def attend(projected, chance, mine, other, first, count, before=None):
    def body(*refs):
        attend_body(*refs[:4], *refs[-3:])

    def block(width):
        return pl.BlockSpec((1024, width), lambda h: (0, h + first))

    more = [] if before is None else [before]
    return pl.pallas_call(
        body,
        grid=(count,),
        in_specs=[block(3 * HEAD), block(1024), block(HEAD), block(HEAD)]
        + [pl.BlockSpec(memory_space=pl.ANY)] * len(more),
        out_specs=block(3 * HEAD),
        out_shape=jax.ShapeDtypeStruct(projected.shape, BF16),
        input_output_aliases={4: 0} if more else {},
        scratch_shapes=[pltpu.VMEM((1024, HEAD), F32)] * 2,
        compiler_params=params(),
        cost_estimate=cost(4 * count),
        name="attend",
    )(projected, chance, mine, other, *more)


def hidden_step_body(
    place, mine_ref, other_ref, slope_a, slope_b, turned_ref, grad_ref, out_a, out_b
):
    for slope_ref, out_ref, at in (
        (slope_a, out_a, slice(0, 384)),
        (slope_b, out_b, slice(384, 768)),
    ):
        total = mine_ref[:, at].astype(F32) + other_ref[:, at].astype(F32)
        grad = (total * slope_ref[...].astype(F32)).astype(BF16)
        grad_ref[:, at] = grad
        out_ref[...] = dot(turned_ref[...], grad, NN).astype(BF16)


def hidden_step(place, steps, mine, other, slope, turned):
    return pl.pallas_call(
        hidden_step_body,
        grid_spec=pltpu.PrefetchScalarGridSpec(
            num_scalar_prefetch=1,
            grid=(1,),
            in_specs=[
                pl.BlockSpec((1024, 768), lambda i, p: (0, 0)),
                pl.BlockSpec((1024, 768), lambda i, p: (0, 0)),
                pl.BlockSpec((1024, 384), lambda i, p: (0, lax.rem(p[2] + steps[0], 4))),
                pl.BlockSpec((1024, 384), lambda i, p: (0, lax.rem(p[2] + steps[1], 4))),
                pl.BlockSpec((384, 1024), lambda i, p: (0, 0)),
            ],
            out_specs=[
                pl.BlockSpec((1024, 768), lambda i, p: (0, 0)),
                pl.BlockSpec((384, 384), lambda i, p: (0, 0)),
                pl.BlockSpec((384, 384), lambda i, p: (0, 0)),
            ],
        ),
        out_shape=(
            jax.ShapeDtypeStruct((1024, 768), BF16),
            jax.ShapeDtypeStruct((384, 384), BF16),
            jax.ShapeDtypeStruct((384, 384), BF16),
        ),
        compiler_params=params(),
        cost_estimate=cost(4),
        name="hidden_step",
    )(place, mine, other, slope, slope, turned)


CUT = (384, 96, 288)


def pack_body(place, hidden_ref, merge_ref, attend_ref, *outs):
    for step in range(4):
        owner, row = lax.rem(place[2] + step, 4), 0
        for ref, size in zip((hidden_ref, merge_ref, attend_ref), CUT, strict=True):
            at = pl.ds(pl.multiple_of(owner * size, 32), size)
            outs[step][row : row + size, :] = ref[at, :]
            row += size


def pack(place, parts):
    return pl.pallas_call(
        pack_body,
        in_specs=[pl.BlockSpec(memory_space=pltpu.SMEM)] + whole(3),
        out_specs=whole(4),
        out_shape=[jax.ShapeDtypeStruct((sum(CUT), 384), BF16)] * 4,
        compiler_params=params(),
        cost_estimate=cost(1),
        name="pack",
    )(place, *parts)


PAIRS = ((2, 1), (3, 0))


def input_body(place, *refs):
    attend_ref, turned, weights, hidden = refs[0], refs[1:5], refs[5:9], refs[9:11]
    out_ref, held = refs[11], refs[12]
    for step in range(4):
        row = lax.rem(place[2] + step, 4) * 288
        held[pl.ds(pl.multiple_of(row, 32), 288), :] = turned[step][384:, :]
    total = dot(attend_ref[...], held[...], NN)
    for which, steps in enumerate(PAIRS):
        for half, step in enumerate(steps):
            total += dot(
                hidden[which][:, half * 384 : half * 384 + 384],
                weights[step][384:, :],
                NT,
            )
    out_ref[...] = total.astype(BF16)


def input_part(place, projected_grad, turned, weights, hidden):
    return pl.pallas_call(
        input_body,
        in_specs=[pl.BlockSpec(memory_space=pltpu.SMEM)] + whole(11),
        out_specs=pl.BlockSpec(memory_space=pltpu.VMEM),
        out_shape=jax.ShapeDtypeStruct((1024, 384), BF16),
        scratch_shapes=[pltpu.VMEM((1152, 384), BF16)],
        compiler_params=params(),
        cost_estimate=cost(5),
        name="input_part",
    )(place, projected_grad, *turned, *weights, *hidden)


def local(
    normed,
    out_grad,
    projected,
    mixed_heads,
    hidden_pre,
    attend_in,
    hidden_in,
    attend_out,
    hidden_out,
):
    across = lax.axis_index("gx")
    place = jnp.stack(
        [across % 4, across // 4, lax.axis_index("gy"), lax.axis_index("gz") // 2]
    ).astype(jnp.int32)

    def over_z(value):
        return lax.all_to_all(
            jnp.broadcast_to(value[None], (4,) + value.shape),
            "gz",
            0,
            0,
            axis_index_groups=[[0, 2, 4, 6], [1, 3, 5, 7]],
        )

    own_rows = jnp.concatenate([out_grad, normed], axis=0)
    beyond = lax.ppermute(own_rows, "gx", Z_LO)
    small = jnp.concatenate([out_grad, beyond[:128], attend_out], axis=0)
    smalls = over_z(small)
    firsts = from_others(
        jnp.concatenate([hidden_out, attend_in.T], axis=0), "gy", Y_NEXT, Y_FAR, Y_PREV
    )
    norms = from_others(
        jnp.concatenate([normed, beyond[128:]], axis=0), "gx", X_NEXT, X_FAR, X_PREV
    )
    pre_float = hidden_pre.astype(F32)
    slope = gelu_slope(pre_float).astype(BF16)
    activated = gelu_value(pre_float).astype(BF16)
    chance = probabilities(projected)
    smalls, weights, firsts, norms, slope, activated, chance = (
        lax.optimization_barrier(
            (smalls, hidden_out, firsts, norms, slope, activated, chance)
        )
    )
    row_piece, head_piece = spread(place, smalls, hidden_in)

    after = lax.ppermute(row_piece, "gx", X_NEXT)
    before = lax.ppermute(row_piece, "gx", X_PREV)
    rows = [
        row_piece,
        after,
        before,
        lax.ppermute(before[:128], "gx", X_PREV),
        lax.ppermute(after[128:], "gx", X_NEXT),
    ]

    others_z = others_of(place, over_z(weights))
    head_weights = from_others(head_piece, "gy", Y_NEXT, Y_FAR, Y_PREV)
    others_z, head_weights, rows = lax.optimization_barrier(
        (others_z, head_weights, rows)
    )
    last_after = lax.ppermute(others_z, "gy", Y_NEXT)
    last_before = lax.ppermute(others_z, "gy", Y_PREV)

    grads = assemble(place, rows)
    normed_slab, turned = assemble_norm(place, norms)
    own_grads = grads[:, :384]
    merge_mine = merge_part(place, grads, head_weights)
    merge_other = lax.ppermute(merge_mine, "gz", CORE)
    projected_grad = attend(projected, chance, merge_mine, merge_other, 0, 2)
    projected_grad, last_after, last_before = lax.optimization_barrier(
        (projected_grad, last_after, last_before)
    )
    last_far = [
        lax.ppermute(last_before[:192], "gy", Y_PREV),
        lax.ppermute(last_after[192:], "gy", Y_NEXT),
    ]
    projected_grad = attend(
        projected, chance, merge_mine, merge_other, 2, 1, projected_grad
    )
    parts = (
        jnp.einsum("tg,td->gd", activated, own_grads, preferred_element_type=F32),
        jnp.einsum("tg,td->gd", mixed_heads, own_grads, preferred_element_type=F32),
        jnp.einsum("tq,td->qd", projected_grad, normed_slab, preferred_element_type=F32),
    )
    chunks = pack(place, [part.astype(BF16) for part in parts])
    last_far, chunks = lax.optimization_barrier((last_far, chunks))

    got = to_owners(chunks)
    mines = [
        hidden_part(grads, [firsts[2], firsts[1]], last_far + [last_after]),
        hidden_part(grads, [firsts[3], firsts[0]], [last_before, others_z]),
    ]
    others = [lax.ppermute(mine, "gz", CORE) for mine in mines]
    hidden, inner_grads = [], [None] * 4
    for which, steps in enumerate(PAIRS):
        grad, inner_grads[steps[0]], inner_grads[steps[1]] = hidden_step(
            place, steps, mines[which], others[which], slope, turned
        )
        hidden.append(grad)
    inner_got = to_owners(inner_grads)

    rows = input_part(place, projected_grad, firsts, head_weights, hidden)
    rows = lax.all_to_all(rows.reshape(8, 128, 384), "gx", 0, 0)
    normed_grad = jnp.sum(rows.astype(F32), axis=0).astype(BF16)
    sums = added(got)
    return normed_grad, sums[480:].T, added(inner_got), sums[384:480], sums[:384]


def solution(mesh):
    placed = (
        P(("gy", "gx"), "gz"),
        P(("gy", "gx"), "gz"),
        P("gy", "gx"),
        P("gy", "gx"),
        P("gy", "gx"),
        P("gz", ("gx", "gy")),
        P("gz", ("gx", "gy")),
        P(("gx", "gy"), "gz"),
        P(("gx", "gy"), "gz"),
    )
    return jax.shard_map(
        local,
        mesh=mesh,
        in_specs=placed,
        out_specs=(
            P(("gy", "gx"), "gz"),
            P("gz", ("gx", "gy")),
            P("gz", ("gx", "gy")),
            P(("gx", "gy"), "gz"),
            P(("gx", "gy"), "gz"),
        ),
        check_vma=False,
    )
```
